256 devices in a mesh: group: 2 (over y_lo), branch: 16 (over y_hi, x, core), tensor: 8 (over z).
Axes of the slice: x: 4, y: 4 (y_hi: 2, y_lo: 2; y = y_hi * 2 + y_lo), z: 8, core: 2. Of those that a mesh axis runs over, the one named last changes fastest.
Arguments:
- queries: bfloat16 [8192, 8192], P(('group', 'branch'), 'tensor'), parts along dimension 0, may hold values from -160 to 160
- prefix_cache: bfloat16 [2, 3072, 1024], P(None, 'group', 'tensor'), parts along dimension 1, may hold values from -5 to 5
- prior_cache: bfloat16 [2, 8192, 1024], P(None, ('group', 'branch'), 'tensor'), parts along dimension 1, may hold values from -5 to 5
- fresh_cache: bfloat16 [2, 8192, 1024], P(None, ('group', 'branch'), 'tensor'), parts along dimension 1, may hold values from -5 to 5
- visible: int32 [32, 16], P('group'), parts along dimension 0, may hold values 0 or 1
- turn_order: int32 [32], P('group'), parts along dimension 0, may hold values from 0 to 15, each once
- output_weight: bfloat16 [8192, 8192], P('tensor', 'branch'), may hold values from -0.0625 to 0.0625
Outputs:
- projected: bfloat16 [8192, 8192], P(('group', 'branch'), 'tensor'), parts along dimension 0
The draws below stay inside these ranges and needn't reach their ends.
There are 2 independent parts, one for each index of `group`. The reference program is written for one: setup_inputs(seed, part) draws one part's arguments, and reference() takes and returns one part's arrays. A program takes and returns all parts, laid end to end along the dimension named above; an argument that names none is the same for every part. Nothing has to cross between parts.
Inputs may be any that keep to these rules, and one draw needn't show every extreme that they name: `turn_order`: each of 0 to 15 once.
All inputs are finite; a program needn't handle non-finite values.
Results may differ from the reference program's by a relative error of at most 0.015.
Values may be sent and summed in bfloat16 or wider, within the bound.
A program may use at most 64 MiB of HBM per device.

```python
import math
import jax
import jax.numpy as jnp
from jax import lax

D = 8192
H = 64
KVH = 8
HD = 128
MSG = 256
PREFIX = 1536
AGENTS = 16
TOKENS = 4096
QW = 8192
KVW = 1024
N_BRANCH = 16
N_TENSOR = 8


def shared_prefix(key):
    base_key = jax.random.fold_in(key, 7)
    cache = jnp.clip(jax.random.normal(jax.random.fold_in(base_key, 1), (2, PREFIX, KVH * HD), jnp.float32), -5.0, 5.0)
    return cache


def draw_prefix_cache(key, part):
    cache = shared_prefix(key)
    return cache.astype(jnp.bfloat16)


def draw_queries(key, part):
    values = jnp.clip(jax.random.normal(jax.random.fold_in(key, 4), (TOKENS, H * HD), jnp.float32) * 2.5, -15.0, 15.0)
    return values.astype(jnp.bfloat16)


def place_ends(result, own_key, low, high):
    longest = result.shape.index(max(result.shape))
    spots = []
    for shift in (0, 1):
        where = [jax.random.randint(jax.random.fold_in(own_key, axis), (), 0, length) for axis, length in enumerate(result.shape)]
        where[longest] = (where[longest] + shift) % result.shape[longest]
        spots.append(tuple(where))
    return result.at[spots[0]].set(low).at[spots[1]].set(high)


def steps_of(key, extent, cuts, smallest, high):
    factor_of, own = 1.0, jax.random.fold_in(key, 6)
    for axis_at, parts in cuts:
        draws = jnp.exp(jax.random.uniform(jax.random.fold_in(own, axis_at), (parts,), jnp.float32, smallest / len(cuts), high / len(cuts)))
        factor_of = factor_of * jnp.repeat(draws, extent[axis_at] // parts).reshape([-1 if axis == axis_at else 1 for axis in range(len(extent))])
    return factor_of


def normal_values(stream_key, shape, spread, most, cuts=(), kind=jnp.bfloat16):
    result = jax.random.normal(stream_key, shape, jnp.float32) * spread
    if len(cuts) > 0:
        result = steps_of(stream_key, shape, cuts, -0.22, 0.18) * result
    return jnp.clip(result, min=-most, max=most).astype(kind)


def setup_inputs(seed: int = 0, part: int = 0) -> dict:
    splits = jax.random.split(jax.random.key(seed), 8)
    own_keys = jax.random.split(jax.random.fold_in(splits[7], part), 8)
    queries = draw_queries(jax.random.fold_in(jax.random.fold_in(splits[7], part), 71), part)
    prefix_cache = draw_prefix_cache(jax.random.fold_in(jax.random.fold_in(splits[7], part), 71), part)
    prior_cache = normal_values(own_keys[2], (2, TOKENS, KVW), 1.0, 5.0, ((1, 16), (2, 8)))
    fresh_cache = normal_values(own_keys[3], (2, TOKENS, KVW), 1.0, 5.0, ((1, 16), (2, 8)))
    visible = place_ends((jax.random.randint(own_keys[4], (AGENTS, AGENTS), 0, 2) < 1).astype(jnp.int32), jax.random.fold_in(own_keys[4], 1), 0, 1)
    turn_order = jax.random.permutation(own_keys[5], AGENTS).astype(jnp.int32)
    output_weight = normal_values(splits[6], (QW, D), QW ** -0.5, 0.0625, ((0, 8), (1, 16)))
    return dict(queries=queries, prefix_cache=prefix_cache, prior_cache=prior_cache, fresh_cache=fresh_cache, visible=visible, turn_order=turn_order, output_weight=output_weight)


NEGATIVE = -1e+30

def reference(queries, prefix_cache, prior_cache, fresh_cache, visible, turn_order, output_weight):
    sharing = H // KVH
    key_rows = jnp.concatenate([prefix_cache[0], prior_cache[0], fresh_cache[0]], axis=0).reshape(-1, KVH, HD)
    value_rows = jnp.concatenate([prefix_cache[1], prior_cache[1], fresh_cache[1]], axis=0).reshape(-1, KVH, HD)
    message_index = jnp.arange(TOKENS, dtype=jnp.int32)
    owner_ids = message_index // MSG
    offsets = message_index % MSG
    positions = jnp.arange(MSG, dtype=jnp.int32)

    def one_agent(agent_id):
        query_rows = lax.dynamic_slice_in_dim(queries, agent_id * MSG, MSG, 0).reshape(MSG, KVH, sharing, HD)
        prior_seen = visible[agent_id][owner_ids] == 1
        fresh_seen = (turn_order[owner_ids] < turn_order[agent_id])[None, :] | (owner_ids == agent_id)[None, :] & (offsets[None, :] <= positions[:, None])
        allowed = jnp.concatenate([jnp.ones((MSG, PREFIX), jnp.bool_), jnp.broadcast_to(prior_seen[None, :], (MSG, TOKENS)), fresh_seen], axis=1)

        def one_group(group_id):
            query_group = lax.dynamic_index_in_dim(query_rows, group_id, 1, False).astype(jnp.float32)
            key_group = lax.dynamic_index_in_dim(key_rows, group_id, 1, False).astype(jnp.float32)
            value_group = lax.dynamic_index_in_dim(value_rows, group_id, 1, False).astype(jnp.float32)
            scores = jnp.einsum('qsd,kd->sqk', query_group, key_group) / math.sqrt(HD)
            masked = jnp.where(allowed[None], scores, NEGATIVE)
            row_peak = lax.optimization_barrier(jnp.max(masked, axis=-1, keepdims=True))
            weights = jnp.where(allowed[None], jnp.exp(masked - row_peak), 0.0)
            row_total = lax.optimization_barrier(jnp.sum(weights, axis=-1, keepdims=True))
            rounded = lax.optimization_barrier(weights.astype(jnp.bfloat16)).astype(jnp.float32)
            return (jnp.einsum('sqk,kd->sqd', rounded, value_group) / row_total).astype(jnp.bfloat16)
        grouped = lax.map(one_group, jnp.arange(KVH, dtype=jnp.int32))
        return jnp.transpose(grouped, (2, 0, 1, 3)).reshape(MSG, H * HD)
    attention = lax.map(one_agent, jnp.arange(AGENTS, dtype=jnp.int32)).reshape(TOKENS, H * HD)
    block_width = H * HD // N_TENSOR

    def add_block(summed, block_index):
        section = lax.dynamic_slice_in_dim(attention, block_index * block_width, block_width, 1)
        weight_rows = lax.dynamic_slice_in_dim(output_weight, block_index * block_width, block_width, 0)
        product = jnp.dot(section, weight_rows, preferred_element_type=jnp.float32)
        return (summed + lax.optimization_barrier(product.astype(jnp.bfloat16)).astype(jnp.float32), None)
    summed, unused = lax.scan(add_block, jnp.zeros((TOKENS, D), jnp.float32), jnp.arange(N_TENSOR, dtype=jnp.int32))
    rounded_sum = summed.astype(jnp.bfloat16)
    piece_width = D // (N_BRANCH * N_TENSOR)
    return jnp.transpose(rounded_sum.reshape(TOKENS, N_BRANCH, N_TENSOR, piece_width), (0, 2, 1, 3)).reshape(TOKENS, D)
```

```python
import math

import jax
import jax.numpy as jnp
from jax import lax
from jax.experimental import pallas as pl
from jax.experimental.pallas import tpu as pltpu
from jax.sharding import PartitionSpec as P

MESH = pl.DeviceIdType.MESH
HD = 128
HEADS = 8
MSG = 256
PREFIX = 1536
CH = 4
ROWS = MSG // CH
QT = ROWS * HEADS
TR = 8
ST = 2 * CH
LAST = 3
SCALE = math.log2(math.e) / math.sqrt(HD)
BIG = 1e30
BF = jnp.bfloat16
F32 = jnp.float32


def dg(a, b, ca, cb):
    return lax.dot_general(a, b, (((ca,), (cb,)), ((), ())), preferred_element_type=F32)


def pick(index, values):
    result = jnp.int32(values[0])
    for i in range(1, len(values)):
        result = jnp.where(index == i, jnp.int32(values[i]), result)
    return result


def kernel(q_ref, pre_ref, pri_ref, fre_ref, vis_ref, turn_ref, w_ref, o_ref,
           qs, pvt, kv, m, acc, ag, wraw, w4, part, rbuf, sbuf, stage,
           kv_s, kv_r, kf_s, kc_s, kc_r, w_s, w_r, wl_s, a_s, a_r, rs_s, rs_r, f_s, f_r):
    b = lax.axis_index("branch")
    z = lax.axis_index("tensor")
    c = lax.rem(b, 2)
    x = lax.rem(b // 2, 4)
    yh = b // 8
    chip = b // 2

    def dev(dy, dx, dc, dz=0):
        ny, nx, nc = lax.rem(yh + dy, 2), lax.rem(x + dx, 4), lax.rem(c + dc, 2)
        return {"branch": (ny * 4 + nx) * 2 + nc, "tensor": lax.rem(z + dz, TR)}

    def chip_at(dy, dx):
        return lax.rem(yh + dy, 2) * 4 + lax.rem(x + dx, 4)

    def remote(src, dst, ss, rs, to):
        return pltpu.make_async_remote_copy(src_ref=src, dst_ref=dst, send_sem=ss, recv_sem=rs,
                                            device_id=to, device_id_type=MESH)

    def put_tile(dst_rows, src):
        kv[chip, c, pl.ds(dst_rows, 128), :] = src

    kv[chip, c, 0:256, :] = pri_ref[0]
    kv[chip, c, 256:512, :] = fre_ref[0]
    for i in range(2):
        kv[chip, c, 512 + i * 128:640 + i * 128, :] = pri_ref[1, i * 128:(i + 1) * 128, :].astype(F32).T.astype(BF)
        kv[chip, c, 768 + i * 128:896 + i * 128, :] = fre_ref[1, i * 128:(i + 1) * 128, :].astype(F32).T.astype(BF)

    barrier = pltpu.get_barrier_semaphore()
    peers = [dev(0, 0, 1), dev(0, 1, 0), dev(0, 3, 0), dev(0, 2, 0), dev(1, 0, 0), dev(0, 0, 0, 1), dev(0, 0, 0, TR - 1)]
    for peer in peers:
        pl.semaphore_signal(barrier, inc=1, device_id=peer, device_id_type=MESH)
    pl.semaphore_wait(barrier, len(peers))

    def kv_send(i):
        to = [dev(0, 1, 0), dev(0, 3, 0), dev(1, 0, 0), dev(0, 2, 0)][i]
        return remote(kv.at[chip, c], kv.at[chip, c], kv_s.at[i], kv_r.at[chip], to)

    across = chip_at(1, 0)

    def kv_forward(i):
        to = [dev(0, 1, 0), dev(0, 3, 0), dev(0, 2, 0)][i]
        return remote(kv.at[across, c], kv.at[across, c], kf_s.at[i], kv_r.at[across], to)

    def kv_arrival(slot):
        return remote(kv.at[slot, c], kv.at[slot, c], kv_s.at[0], kv_r.at[slot], dev(0, 1, 0))

    def core_send(slot):
        return remote(kv.at[slot, c], kv.at[slot, c], kc_s.at[slot], kc_r.at[slot], dev(0, 0, 1))

    def core_arrival(slot):
        return remote(kv.at[slot, 1 - c], kv.at[slot, 1 - c], kc_s.at[slot], kc_r.at[slot], dev(0, 0, 1))

    core_send(chip).start()
    kv_send(0).start()
    kv_send(1).start()
    kv_send(2).start()

    own_w = yh * 2 + c
    far_w = (1 - yh) * 2 + c
    w_local = pltpu.make_async_copy(w_ref, wraw.at[own_w], wl_s.at[0])
    w_across = remote(w_ref, wraw.at[own_w], w_s.at[0], w_r.at[0], dev(1, 0, 0))
    w_core = remote(w_ref, wraw.at[own_w], w_s.at[1], w_r.at[1], dev(0, 0, 1))
    w_pass = remote(wraw.at[far_w], wraw.at[far_w], w_s.at[2], w_r.at[2], dev(0, 0, 1))
    w_local.start()

    for j in range(CH):
        for h in range(HEADS):
            qs[j, h * ROWS:(h + 1) * ROWS, :] = q_ref[j * ROWS:(j + 1) * ROWS, h * HD:(h + 1) * HD]
    for i in range(PREFIX // 128):
        pvt[i] = pre_ref[1, i * 128:(i + 1) * 128, :].astype(F32).T.astype(BF)
    m[...] = jnp.full(m.shape, -BIG, F32)
    acc[...] = jnp.zeros(acc.shape, F32)

    def scores(keys, j):
        return dg(keys, qs[j], 1, 1)

    def with_ones(tiles):
        values = jnp.concatenate(tiles, axis=1)
        return jnp.concatenate([values, jnp.ones((16, values.shape[1]), BF)], axis=0)

    def soften(j, s, values, sections):
        old = m[j]
        new = old
        parts = []
        for start, size, penalty, limit in sections:
            sec = s[start:start + size]
            if limit is not None:
                row = lax.broadcasted_iota(jnp.int32, sec.shape, 0)
                sec = jnp.where(row <= limit, sec, -BIG)
            top = jnp.max(sec, axis=0, keepdims=True) * SCALE
            if penalty is not None:
                top = top - penalty
            new = jnp.maximum(new, top)
            parts.append((sec, penalty))
        weights = []
        for sec, penalty in parts:
            shift = new if penalty is None else new + penalty
            weights.append(jnp.exp2(sec * SCALE - shift).astype(BF))
        p = weights[0] if len(weights) == 1 else jnp.concatenate(weights, axis=0)
        m[j] = new
        acc[j] = acc[j] * jnp.exp2(old - new) + dg(values, p, 1, 0)

    def sweep(keys, values, sections_of):
        ahead = scores(keys, 0)
        for j in range(CH):
            s = ahead
            if j + 1 < CH:
                ahead = scores(keys, j + 1)
            soften(j, s, values, sections_of(j))

    my_turn = turn_ref[b]

    def chip_keys(slot):
        return jnp.concatenate([kv[slot, 0, 0:512, :], kv[slot, 1, 0:512, :]], axis=0)

    def chip_values(slot):
        return with_ones([kv[slot, cc, 512 + 128 * i:640 + 128 * i, :] for cc in range(2) for i in range(4)])

    def chip_sections(slot, limits=None):
        out = []
        for cc in range(2):
            owner = slot * 2 + cc
            unseen = jnp.where(vis_ref[b, owner] == 1, 0.0, BIG)
            early = turn_ref[owner] < my_turn
            if limits is not None:
                early = early | (owner == b)
            later = jnp.where(early, 0.0, BIG)
            out.append((cc * 512, 256, unseen, None))
            out.append((cc * 512 + 256, 256, later, None if limits is None else limits[cc]))
        return out

    sweep(pre_ref[0], with_ones([pvt[i] for i in range(PREFIX // 128)]), lambda j: [(0, PREFIX, None, None)])

    kv_send(3).start()
    kv_arrival(across).wait_recv()
    kv_forward(0).start()
    kv_forward(1).start()
    core_send(across).start()
    w_core.start()
    w_across.start()
    core_arrival(chip).wait_recv()

    def own_sections(j):
        position = lax.rem(lax.broadcasted_iota(jnp.int32, (1, QT), 1), ROWS) + j * ROWS
        limits = [position + jnp.where(chip * 2 + cc == b, 0, MSG) for cc in range(2)]
        return chip_sections(chip, limits)

    sweep(chip_keys(chip), chip_values(chip), own_sections)
    kv_forward(2).start()

    order = [(0, 1), (0, 3), (1, 0), (0, 2), (1, 1), (1, 3), (1, 2)]
    FIRST = len(order) - LAST

    def slot_of(s):
        return chip_at(pick(s, [p[0] for p in order]), pick(s, [p[1] for p in order]))

    def fetch(s):
        @pl.when(s != 2)
        def _():
            slot = slot_of(s)
            kv_arrival(slot).wait_recv()
            core_send(slot).start()

    fetch(jnp.int32(0))

    def first_part(s, carry):
        slot = slot_of(s)
        fetch(s + 1)
        core_arrival(slot).wait_recv()
        sweep(chip_keys(slot), chip_values(slot), lambda j: chip_sections(slot))
        return carry

    lax.fori_loop(0, FIRST, first_part, 0)

    for s in range(FIRST + 1, len(order)):
        fetch(jnp.int32(s))
    for s in range(FIRST, len(order)):
        core_arrival(slot_of(jnp.int32(s))).wait_recv()

    def arrange(y):
        def some_rows(i, carry):
            rows = pl.ds(pl.multiple_of(i * 128, 128), 128)
            for u in range(4):
                low = wraw[y * 2, rows, u * 128:(u + 1) * 128]
                high = wraw[y * 2 + 1, rows, u * 128:(u + 1) * 128]
                w4[y, rows, u * 256:u * 256 + 128] = jnp.concatenate([low[:, :64], high[:, :64]], axis=1)
                w4[y, rows, u * 256 + 128:u * 256 + 256] = jnp.concatenate([low[:, 64:], high[:, 64:]], axis=1)
            return carry
        lax.fori_loop(0, 8, some_rows, 0)

    w_local.wait()
    w_core.wait_recv()
    arrange(yh)

    def a_send(j, r):
        return remote(ag.at[j, x], ag.at[j, x], a_s.at[j, r - 1], a_r.at[j, r - 1], dev(0, r, 0))

    last_slots = [slot_of(jnp.int32(s)) for s in range(FIRST, len(order))]

    def second_part(j, carry):
        ahead = scores(chip_keys(last_slots[0]), j)
        for n in range(LAST):
            s = ahead
            if n + 1 < LAST:
                ahead = scores(chip_keys(last_slots[n + 1]), j)
            soften(j, s, chip_values(last_slots[n]), chip_sections(last_slots[n]))
        done = acc[j]
        heads = (done[:HD] / done[HD:HD + 1]).T.astype(BF)
        for h in range(HEADS):
            ag[j, x, :, h * HD:(h + 1) * HD] = heads[h * ROWS:(h + 1) * ROWS, :]
        for r in (1, 3, 2):
            a_send(j, r).start()

        @pl.when(j == CH - 2)
        def _():
            w_across.wait_recv()
            w_pass.start()

        return carry

    lax.fori_loop(0, CH, second_part, 0)

    def ring_copy(st, s, d):
        to = dev(0, 0, 0, 1 if d == 0 else TR - 1)
        return remote(sbuf.at[st, s, d], rbuf.at[st, s, d], rs_s.at[st, s, d], rs_r.at[st, s, d], to)

    def target(s, d):
        return lax.rem(z + 2 * TR - 1 - s, TR) if d == 0 else lax.rem(z + 1 + s, TR)

    def final_send(st, r):
        j, y = st // 2, lax.rem(yh + st, 2)
        spot = o_ref.at[pl.ds(pl.multiple_of(j * ROWS, ROWS), ROWS), pl.ds(pl.multiple_of((y * 4 + x) * 128, 128), 128)]
        return remote(stage.at[st, lax.rem(x + r, 4)], spot, f_s.at[st, r - 1], f_r.at[st, r - 1], dev(0, r, 0))

    def final_arrival(st, r):
        j, y = st // 2, lax.rem(yh + st, 2)
        source = lax.rem(x + 4 - r, 4)
        spot = o_ref.at[pl.ds(pl.multiple_of(j * ROWS, ROWS), ROWS), pl.ds(pl.multiple_of((y * 4 + source) * 128, 128), 128)]
        return remote(stage.at[st, 0], spot, f_s.at[st, r - 1], f_r.at[st, r - 1], dev(0, r, 0))

    def begin(st):
        j, y = st // 2, lax.rem(yh + st, 2)

        @pl.when(lax.rem(st, 2) == 0)
        def _():
            for r in (1, 3, 2):
                source = lax.rem(x + 4 - r, 4)
                remote(ag.at[j, source], ag.at[j, source], a_s.at[j, r - 1], a_r.at[j, r - 1], dev(0, r, 0)).wait_recv()

        @pl.when(st == 1)
        def _():
            w_pass.wait_recv()
            arrange(1 - yh)

        left = ag[j].reshape(4 * ROWS, HEADS * HD)
        for u in range(4):
            product = dg(left, w4[y, :, u * 256:(u + 1) * 256], 1, 0).astype(BF)
            part[st, 2 * u] = product[:, :128]
            part[st, 2 * u + 1] = product[:, 128:]
        for d in range(2):
            sbuf[st, 0, d] = part[st, target(0, d), d * 128:(d + 1) * 128, :]
            ring_copy(st, 0, d).start()

    def middle(st, s):
        for d in range(2):
            ring_copy(st, s - 1, d).wait_recv()
            total = rbuf[st, s - 1, d].astype(F32) + part[st, target(s, d), d * 128:(d + 1) * 128, :].astype(F32)
            sbuf[st, s, d] = total.astype(BF)
            ring_copy(st, s, d).start()

    def finish(st):
        j, y = st // 2, lax.rem(yh + st, 2)
        for d in range(2):
            ring_copy(st, TR - 2, d).wait_recv()
            total = rbuf[st, TR - 2, d].astype(F32) + part[st, z, d * 128:(d + 1) * 128, :].astype(F32)
            stage[st, 2 * d:2 * d + 2] = total.astype(BF).reshape(2, ROWS, 128)
        for r in (1, 3, 2):
            final_send(st, r).start()
        o_ref[pl.ds(pl.multiple_of(j * ROWS, ROWS), ROWS), pl.ds(pl.multiple_of((y * 4 + x) * 128, 128), 128)] = stage[st, x]

    def tick(T, carry):
        def one(st, inner):
            s = T - st

            @pl.when(s == 0)
            def _():
                begin(st)

            @pl.when((s >= 1) & (s < TR - 1))
            def _():
                middle(st, s)

            @pl.when(s == TR - 1)
            def _():
                finish(st)

            return inner

        return lax.fori_loop(0, ST, one, carry)

    lax.fori_loop(0, ST + TR - 1, tick, 0)

    def drain(st, carry):
        for r in (1, 2, 3):
            final_arrival(st, r).wait_recv()
            final_send(st, r).wait_send()
        return carry

    lax.fori_loop(0, ST, drain, 0)

    def drain_ring(n, carry):
        for d in range(2):
            ring_copy(n // (TR - 1), lax.rem(n, TR - 1), d).wait_send()
        return carry

    lax.fori_loop(0, ST * (TR - 1), drain_ring, 0)

    def drain_heads(j, carry):
        for r in (1, 2, 3):
            a_send(j, r).wait_send()
        return carry

    lax.fori_loop(0, CH, drain_heads, 0)
    for i in range(4):
        kv_send(i).wait_send()
    for i in range(3):
        kv_forward(i).wait_send()

    def drain_core(slot, carry):
        core_send(slot).wait_send()
        return carry

    lax.fori_loop(0, 8, drain_core, 0)
    w_across.wait_send()
    w_core.wait_send()
    w_pass.wait_send()


def per_device(queries, prefix_cache, prior_cache, fresh_cache, visible, turn_order, output_weight):
    vm = pl.BlockSpec(memory_space=pltpu.VMEM)
    sm = pl.BlockSpec(memory_space=pltpu.SMEM)
    dma = pltpu.SemaphoreType.DMA
    return pl.pallas_call(
        kernel,
        name="debate",
        out_shape=jax.ShapeDtypeStruct(queries.shape, BF),
        in_specs=[vm, vm, vm, vm, sm, sm, vm],
        out_specs=vm,
        scratch_shapes=[
            pltpu.VMEM((CH, QT, HD), BF),
            pltpu.VMEM((PREFIX // 128, 128, 128), BF),
            pltpu.VMEM((8, 2, 1024, HD), BF),
            pltpu.VMEM((CH, 1, QT), F32),
            pltpu.VMEM((CH, HD + 16, QT), F32),
            pltpu.VMEM((CH, 4, ROWS, HEADS * HD), BF),
            pltpu.VMEM((4, 1024, 512), BF),
            pltpu.VMEM((2, 1024, 1024), BF),
            pltpu.VMEM((ST, TR, 4 * ROWS, 128), BF),
            pltpu.VMEM((ST, TR - 1, 2, 2 * ROWS, 128), BF),
            pltpu.VMEM((ST, TR - 1, 2, 2 * ROWS, 128), BF),
            pltpu.VMEM((ST, 4, ROWS, 128), BF),
            dma((4,)), dma((8,)), dma((3,)), dma((8,)), dma((8,)),
            dma((3,)), dma((3,)), dma((1,)),
            dma((CH, 3)), dma((CH, 3)),
            dma((ST, TR - 1, 2)), dma((ST, TR - 1, 2)),
            dma((ST, 3)), dma((ST, 3)),
        ],
        compiler_params=pltpu.CompilerParams(collective_id=0, has_side_effects=True, vmem_limit_bytes=60 << 20),
        cost_estimate=pl.CostEstimate(flops=15_000_000_000, bytes_accessed=6_000_000, transcendentals=20_000_000),
    )(queries, prefix_cache, prior_cache, fresh_cache, visible, turn_order, output_weight)


def solution(mesh):
    return jax.shard_map(
        per_device,
        mesh=mesh,
        in_specs=(
            P(("group", "branch"), "tensor"),
            P(None, "group", "tensor"),
            P(None, ("group", "branch"), "tensor"),
            P(None, ("group", "branch"), "tensor"),
            P("group", None),
            P("group"),
            P("tensor", "branch"),
        ),
        out_specs=P(("group", "branch"), "tensor"),
        check_vma=False,
    )
```

```python
import math

import jax
import jax.numpy as jnp
from jax import lax
from jax.experimental import pallas as pl
from jax.experimental.pallas import tpu as pltpu
from jax.sharding import PartitionSpec as P

MESH = pl.DeviceIdType.MESH
HD = 128
HEADS = 8
MSG = 256
PREFIX = 1536
CH = 4
ROWS = MSG // CH
QT = ROWS * HEADS
TR = 8
ST = 2 * CH
START = (0, 1, 2, 2, 2, 3, 3, 3)
SCALE = math.log2(math.e) / math.sqrt(HD)
BIG = 1e30
BF = jnp.bfloat16
F32 = jnp.float32


def dg(a, b, ca, cb):
    return lax.dot_general(a, b, (((ca,), (cb,)), ((), ())), preferred_element_type=F32)


def pick(index, values):
    result = jnp.int32(values[0])
    for i in range(1, len(values)):
        result = jnp.where(index == i, jnp.int32(values[i]), result)
    return result


def kernel(q_ref, pre_ref, pri_ref, fre_ref, vis_ref, turn_ref, w_ref, o_ref,
           qs, pvt, kv, m, acc, ag, wraw, w4, part, rbuf, sbuf, stage,
           kv_s, kv_r, kf_s, kh_s, kh_r, kc_s, kc_r, w_s, w_r, wl_s, a_s, a_r, rs_s, rs_r, f_s, f_r):
    b = lax.axis_index("branch")
    z = lax.axis_index("tensor")
    c = lax.rem(b, 2)
    x = lax.rem(b // 2, 4)
    yh = b // 8
    chip = b // 2

    def dev(dy, dx, dc, dz=0):
        ny, nx, nc = lax.rem(yh + dy, 2), lax.rem(x + dx, 4), lax.rem(c + dc, 2)
        return {"branch": (ny * 4 + nx) * 2 + nc, "tensor": lax.rem(z + dz, TR)}

    def chip_at(dy, dx):
        return lax.rem(yh + dy, 2) * 4 + lax.rem(x + dx, 4)

    def remote(src, dst, ss, rs, to):
        return pltpu.make_async_remote_copy(src_ref=src, dst_ref=dst, send_sem=ss, recv_sem=rs,
                                            device_id=to, device_id_type=MESH)

    barrier = pltpu.get_barrier_semaphore()
    peers = [dev(0, 0, 1), dev(0, 1, 0), dev(0, 3, 0), dev(0, 2, 0), dev(1, 0, 0), dev(0, 0, 0, 1), dev(0, 0, 0, TR - 1)]
    for peer in peers:
        pl.semaphore_signal(barrier, inc=1, device_id=peer, device_id_type=MESH)

    kv[chip, c, 0:256, :] = pri_ref[0]
    kv[chip, c, 256:512, :] = fre_ref[0]
    for i in range(2):
        kv[chip, c, 512 + i * 128:640 + i * 128, :] = pri_ref[1, i * 128:(i + 1) * 128, :].astype(F32).T.astype(BF)
        kv[chip, c, 768 + i * 128:896 + i * 128, :] = fre_ref[1, i * 128:(i + 1) * 128, :].astype(F32).T.astype(BF)

    across = chip_at(1, 0)
    right, left = dev(0, 1, 0), dev(0, 3, 0)
    right_chip, left_chip, far_chip = chip_at(0, 1), chip_at(0, 3), chip_at(0, 2)
    right_across, left_across, far_across = chip_at(1, 1), chip_at(1, 3), chip_at(1, 2)
    halves = (pl.ds(0, 512), pl.ds(512, 512))

    def kv_send(i):
        to = [right, left, dev(1, 0, 0)][i]
        return remote(kv.at[chip, c], kv.at[chip, c], kv_s.at[i], kv_r.at[chip], to)

    def kv_forward(i):
        return remote(kv.at[across, c], kv.at[across, c], kf_s.at[i], kv_r.at[across], [right, left][i])

    def kv_arrival(slot):
        return remote(kv.at[slot, c], kv.at[slot, c], kv_s.at[0], kv_r.at[slot], right)

    def kv_relay(row, half):
        slot = [[left_chip, right_chip], [left_across, right_across]][row][half]
        spot = kv.at[slot, c, halves[half]]
        return remote(spot, spot, kh_s.at[row, half], kh_r.at[row, half], [right, left][half])

    def relay_arrival(row, half):
        spot = kv.at[[far_chip, far_across][row], c, halves[half]]
        return remote(spot, spot, kh_s.at[row, half], kh_r.at[row, half], right)

    def core_send(slot):
        return remote(kv.at[slot, c], kv.at[slot, c], kc_s.at[slot], kc_r.at[slot], dev(0, 0, 1))

    def core_arrival(slot):
        return remote(kv.at[slot, 1 - c], kv.at[slot, 1 - c], kc_s.at[slot], kc_r.at[slot], dev(0, 0, 1))

    own_w = yh * 2 + c
    far_w = (1 - yh) * 2 + c
    w_local = pltpu.make_async_copy(w_ref, wraw.at[own_w], wl_s.at[0])
    w_core = remote(w_ref, wraw.at[own_w], w_s.at[0], w_r.at[0], dev(0, 0, 1))

    def w_across(half):
        return remote(w_ref.at[halves[half]], wraw.at[own_w, halves[half]], w_s.at[1 + half], w_r.at[1 + half], dev(1, 0, 0))

    def w_pass(half):
        spot = wraw.at[far_w, halves[half]]
        return remote(spot, spot, w_s.at[3 + half], w_r.at[3 + half], dev(0, 0, 1))

    w_local.start()

    for j in range(CH):
        for h in range(HEADS):
            qs[j, h * ROWS:(h + 1) * ROWS, :] = q_ref[j * ROWS:(j + 1) * ROWS, h * HD:(h + 1) * HD]
    for i in range(PREFIX // 128):
        pvt[i] = pre_ref[1, i * 128:(i + 1) * 128, :].astype(F32).T.astype(BF)
    m[...] = jnp.full(m.shape, -BIG, F32)
    acc[...] = jnp.zeros(acc.shape, F32)

    def scores(keys, j):
        return dg(keys, qs[j], 1, 1)

    def with_ones(tiles):
        values = jnp.concatenate(tiles, axis=1)
        return jnp.concatenate([values, jnp.ones((16, values.shape[1]), BF)], axis=0)

    def soften(j, s, values, sections):
        old = m[j]
        new = old
        parts = []
        for start, size, penalty, limit in sections:
            sec = s[start:start + size]
            if limit is not None:
                row = lax.broadcasted_iota(jnp.int32, sec.shape, 0)
                sec = jnp.where(row <= limit, sec, -BIG)
            top = jnp.max(sec, axis=0, keepdims=True) * SCALE
            if penalty is not None:
                top = top - penalty
            new = jnp.maximum(new, top)
            parts.append((sec, penalty))
        weights = []
        for sec, penalty in parts:
            shift = new if penalty is None else new + penalty
            weights.append(jnp.exp2(sec * SCALE - shift).astype(BF))
        p = weights[0] if len(weights) == 1 else jnp.concatenate(weights, axis=0)
        m[j] = new
        acc[j] = acc[j] * jnp.exp2(old - new) + dg(values, p, 1, 0)

    def run(items):
        ahead = None
        for n, (before, keys, values, sections, j) in enumerate(items):
            if n == 0:
                before()
                ahead = scores(keys(), j)
            s = ahead
            if n + 1 < len(items):
                items[n + 1][0]()
                ahead = scores(items[n + 1][1](), items[n + 1][4])
            soften(j, s, values(), sections())

    def nothing():
        return None

    my_turn = turn_ref[b]

    def chip_keys(slot):
        return jnp.concatenate([kv[slot, 0, 0:512, :], kv[slot, 1, 0:512, :]], axis=0)

    def chip_values(slot):
        return with_ones([kv[slot, cc, 512 + 128 * i:640 + 128 * i, :] for cc in range(2) for i in range(4)])

    def chip_sections(slot, limits=None):
        out = []
        for cc in range(2):
            owner = slot * 2 + cc
            unseen = jnp.where(vis_ref[b, owner] == 1, 0.0, BIG)
            early = turn_ref[owner] < my_turn
            if limits is not None:
                early = early | (owner == b)
            later = jnp.where(early, 0.0, BIG)
            out.append((cc * 512, 256, unseen, None))
            out.append((cc * 512 + 256, 256, later, None if limits is None else limits[cc]))
        return out

    def prefix_values():
        return with_ones([pvt[i] for i in range(PREFIX // 128)])

    run([(nothing, lambda: pre_ref[0], prefix_values, lambda: [(0, PREFIX, None, None)], j) for j in range(CH)])

    pl.semaphore_wait(barrier, len(peers))
    core_send(chip).start()
    kv_send(0).start()
    kv_send(1).start()
    kv_send(2).start()
    w_core.start()
    core_arrival(chip).wait_recv()

    def own_sections(j):
        position = lax.rem(lax.broadcasted_iota(jnp.int32, (1, QT), 1), ROWS) + j * ROWS
        limits = [position + jnp.where(chip * 2 + cc == b, 0, MSG) for cc in range(2)]
        return chip_sections(chip, limits)

    def arrange(y):
        def some_rows(i, carry):
            rows = pl.ds(pl.multiple_of(i * 128, 128), 128)
            for u in range(4):
                low = wraw[y * 2, rows, u * 128:(u + 1) * 128]
                high = wraw[y * 2 + 1, rows, u * 128:(u + 1) * 128]
                w4[y, rows, u * 256:u * 256 + 128] = jnp.concatenate([low[:, :64], high[:, :64]], axis=1)
                w4[y, rows, u * 256 + 128:u * 256 + 256] = jnp.concatenate([low[:, 64:], high[:, 64:]], axis=1)
            return carry
        lax.fori_loop(0, 8, some_rows, 0)

    def chip_items(slot, sections, before=nothing):
        return [(before if j == 0 else nothing, lambda: chip_keys(slot), lambda: chip_values(slot), lambda j=j: sections(j), j)
                for j in range(CH)]

    run(chip_items(chip, own_sections))
    w_local.wait()
    w_core.wait_recv()
    arrange(yh)

    kv_arrival(right_chip).wait_recv()
    kv_relay(0, 1).start()
    core_send(right_chip).start()
    kv_arrival(left_chip).wait_recv()
    kv_relay(0, 0).start()
    core_send(left_chip).start()
    kv_arrival(across).wait_recv()
    kv_forward(0).start()
    kv_forward(1).start()
    core_send(across).start()
    for half in range(2):
        w_across(half).start()
    core_arrival(right_chip).wait_recv()

    def before_left():
        for half in range(2):
            relay_arrival(0, half).wait_recv()
        core_send(far_chip).start()
        core_arrival(left_chip).wait_recv()

    def before_across():
        core_arrival(across).wait_recv()
        kv_arrival(right_across).wait_recv()
        kv_relay(1, 1).start()
        core_send(right_across).start()
        kv_arrival(left_across).wait_recv()
        kv_relay(1, 0).start()
        core_send(left_across).start()

    run(chip_items(right_chip, lambda j: chip_sections(right_chip))
        + chip_items(left_chip, lambda j: chip_sections(left_chip), before_left)
        + chip_items(across, lambda j: chip_sections(across), before_across))

    for slot in (far_chip, right_across, left_across):
        core_arrival(slot).wait_recv()

    def a_send(j, r):
        return remote(ag.at[j, x], ag.at[j, x], a_s.at[j, r - 1], a_r.at[j, r - 1], dev(0, r, 0))

    def ring_copy(st, s, d):
        to = dev(0, 0, 0, 1 if d == 0 else TR - 1)
        return remote(sbuf.at[st, s, d], rbuf.at[st, s, d], rs_s.at[st, s, d], rs_r.at[st, s, d], to)

    def target(s, d):
        return lax.rem(z + 2 * TR - 1 - s, TR) if d == 0 else lax.rem(z + 1 + s, TR)

    def final_send(st, r):
        j, y = st // 2, lax.rem(yh + st, 2)
        spot = o_ref.at[pl.ds(pl.multiple_of(j * ROWS, ROWS), ROWS), pl.ds(pl.multiple_of((y * 4 + x) * 128, 128), 128)]
        return remote(stage.at[st, lax.rem(x + r, 4)], spot, f_s.at[st, r - 1], f_r.at[st, r - 1], dev(0, r, 0))

    def final_arrival(st, r):
        j, y = st // 2, lax.rem(yh + st, 2)
        source = lax.rem(x + 4 - r, 4)
        spot = o_ref.at[pl.ds(pl.multiple_of(j * ROWS, ROWS), ROWS), pl.ds(pl.multiple_of((y * 4 + source) * 128, 128), 128)]
        return remote(stage.at[st, 0], spot, f_s.at[st, r - 1], f_r.at[st, r - 1], dev(0, r, 0))

    def begin(st):
        j, y = st // 2, lax.rem(yh + st, 2)

        @pl.when(lax.rem(st, 2) == 0)
        def _():
            for r in (1, 3, 2):
                source = lax.rem(x + 4 - r, 4)
                remote(ag.at[j, source], ag.at[j, source], a_s.at[j, r - 1], a_r.at[j, r - 1], dev(0, r, 0)).wait_recv()

        @pl.when(st == 1)
        def _():
            w_pass(0).wait_recv()
            w_pass(1).wait_recv()
            arrange(1 - yh)

        left = ag[j].reshape(4 * ROWS, HEADS * HD)
        for u in range(4):
            product = dg(left, w4[y, :, u * 256:(u + 1) * 256], 1, 0).astype(BF)
            part[st, 2 * u] = product[:, :128]
            part[st, 2 * u + 1] = product[:, 128:]
        for d in range(2):
            sbuf[st, 0, d] = part[st, target(0, d), d * 128:(d + 1) * 128, :]
            ring_copy(st, 0, d).start()

    def middle(st, s):
        for d in range(2):
            ring_copy(st, s - 1, d).wait_recv()
            total = rbuf[st, s - 1, d].astype(F32) + part[st, target(s, d), d * 128:(d + 1) * 128, :].astype(F32)
            sbuf[st, s, d] = total.astype(BF)
            ring_copy(st, s, d).start()

    def finish(st):
        j, y = st // 2, lax.rem(yh + st, 2)
        for d in range(2):
            ring_copy(st, TR - 2, d).wait_recv()
            total = rbuf[st, TR - 2, d].astype(F32) + part[st, z, d * 128:(d + 1) * 128, :].astype(F32)
            stage[st, 2 * d:2 * d + 2] = total.astype(BF).reshape(2, ROWS, 128)
        for r in (1, 3, 2):
            final_send(st, r).start()
        o_ref[pl.ds(pl.multiple_of(j * ROWS, ROWS), ROWS), pl.ds(pl.multiple_of((y * 4 + x) * 128, 128), 128)] = stage[st, x]

    def tick(T, carry):
        def one(st, inner):
            s = T - pick(st, START)

            @pl.when(s == 0)
            def _():
                begin(st)

            @pl.when((s >= 1) & (s < TR - 1))
            def _():
                middle(st, s)

            @pl.when(s == TR - 1)
            def _():
                finish(st)

            return inner

        return lax.fori_loop(0, ST, one, carry)

    def before_second(j):
        @pl.when(j == 0)
        def _():
            for half in range(2):
                relay_arrival(1, half).wait_recv()
            core_send(far_across).start()

        @pl.when(j == CH - 1)
        def _():
            tick(0, 0)

    def before_third(j):
        return None

    def before_last(j):
        @pl.when(j == 0)
        def _():
            core_arrival(far_across).wait_recv()

        @pl.when(j == CH - 1)
        def _():
            tick(1, 0)

    def second_part(j, carry):
        def item(slot, before):
            return (lambda: before(j), lambda: chip_keys(slot), lambda: chip_values(slot), lambda: chip_sections(slot), j)

        run([item(far_chip, lambda j: None), item(left_across, before_second), item(right_across, before_third),
             item(far_across, before_last)])
        done = acc[j]
        heads = (done[:HD] / done[HD:HD + 1]).T.astype(BF)
        for h in range(HEADS):
            ag[j, x, :, h * HD:(h + 1) * HD] = heads[h * ROWS:(h + 1) * ROWS, :]
        for r in (1, 3, 2):
            a_send(j, r).start()
        for half in range(2):
            @pl.when(j == 1 + half)
            def _():
                w_across(half).wait_recv()
                w_pass(half).start()

        return carry

    lax.fori_loop(0, CH, second_part, 0)
    lax.fori_loop(2, START[-1] + TR, tick, 0)

    def drain(st, carry):
        for r in (1, 2, 3):
            final_arrival(st, r).wait_recv()
            final_send(st, r).wait_send()
        return carry

    lax.fori_loop(0, ST, drain, 0)

    def drain_ring(n, carry):
        for d in range(2):
            ring_copy(n // (TR - 1), lax.rem(n, TR - 1), d).wait_send()
        return carry

    lax.fori_loop(0, ST * (TR - 1), drain_ring, 0)

    def drain_heads(j, carry):
        for r in (1, 2, 3):
            a_send(j, r).wait_send()
        return carry

    lax.fori_loop(0, CH, drain_heads, 0)
    for i in range(3):
        kv_send(i).wait_send()
    for i in range(2):
        kv_forward(i).wait_send()
        w_across(i).wait_send()
        w_pass(i).wait_send()
        for row in range(2):
            kv_relay(row, i).wait_send()

    def drain_core(slot, carry):
        core_send(slot).wait_send()
        return carry

    lax.fori_loop(0, 8, drain_core, 0)
    w_core.wait_send()


def per_device(queries, prefix_cache, prior_cache, fresh_cache, visible, turn_order, output_weight):
    vm = pl.BlockSpec(memory_space=pltpu.VMEM)
    sm = pl.BlockSpec(memory_space=pltpu.SMEM)
    dma = pltpu.SemaphoreType.DMA
    return pl.pallas_call(
        kernel,
        name="debate",
        out_shape=jax.ShapeDtypeStruct(queries.shape, BF),
        in_specs=[vm, vm, vm, vm, sm, sm, vm],
        out_specs=vm,
        scratch_shapes=[
            pltpu.VMEM((CH, QT, HD), BF),
            pltpu.VMEM((PREFIX // 128, 128, 128), BF),
            pltpu.VMEM((8, 2, 1024, HD), BF),
            pltpu.VMEM((CH, 1, QT), F32),
            pltpu.VMEM((CH, HD + 16, QT), F32),
            pltpu.VMEM((CH, 4, ROWS, HEADS * HD), BF),
            pltpu.VMEM((4, 1024, 512), BF),
            pltpu.VMEM((2, 1024, 1024), BF),
            pltpu.VMEM((ST, TR, 4 * ROWS, 128), BF),
            pltpu.VMEM((ST, TR - 1, 2, 2 * ROWS, 128), BF),
            pltpu.VMEM((ST, TR - 1, 2, 2 * ROWS, 128), BF),
            pltpu.VMEM((ST, 4, ROWS, 128), BF),
            dma((3,)), dma((8,)), dma((2,)), dma((2, 2)), dma((2, 2)), dma((8,)), dma((8,)),
            dma((5,)), dma((5,)), dma((1,)),
            dma((CH, 3)), dma((CH, 3)),
            dma((ST, TR - 1, 2)), dma((ST, TR - 1, 2)),
            dma((ST, 3)), dma((ST, 3)),
        ],
        compiler_params=pltpu.CompilerParams(collective_id=0, has_side_effects=True, vmem_limit_bytes=60 << 20),
        cost_estimate=pl.CostEstimate(flops=15_000_000_000, bytes_accessed=6_000_000, transcendentals=20_000_000),
    )(queries, prefix_cache, prior_cache, fresh_cache, visible, turn_order, output_weight)


def solution(mesh):
    return jax.shard_map(
        per_device,
        mesh=mesh,
        in_specs=(
            P(("group", "branch"), "tensor"),
            P(None, "group", "tensor"),
            P(None, ("group", "branch"), "tensor"),
            P(None, ("group", "branch"), "tensor"),
            P("group", None),
            P("group"),
            P("tensor", "branch"),
        ),
        out_specs=P(("group", "branch"), "tensor"),
        check_vma=False,
    )
```

```python
import math

import jax
import jax.numpy as jnp
from jax import lax
from jax.experimental import pallas as pl
from jax.experimental.pallas import tpu as pltpu
from jax.sharding import PartitionSpec as P

MESH = pl.DeviceIdType.MESH
HD = 128
HEADS = 8
MSG = 256
PREFIX = 1536
CH = 4
ROWS = MSG // CH
QT = ROWS * HEADS
TR = 8
ST = 2 * CH
START = (0, 1, 2, 2, 2, 2, 3, 3)
SCALE = math.log2(math.e) / math.sqrt(HD)
BIG = 1e30
BF = jnp.bfloat16
F32 = jnp.float32


def dg(a, b, ca, cb):
    return lax.dot_general(a, b, (((ca,), (cb,)), ((), ())), preferred_element_type=F32)


def pick(index, values):
    result = jnp.int32(values[0])
    for i in range(1, len(values)):
        result = jnp.where(index == i, jnp.int32(values[i]), result)
    return result


def kernel(q_ref, pre_ref, pri_ref, fre_ref, vis_ref, turn_ref, w_ref, o_ref,
           qs, pvt, kv, m, acc, ag, wraw, w4, part, rbuf, sbuf, stage,
           kv_s, kv_r, kf_s, kh_s, kh_r, kc_s, kc_r, w_s, w_r, wl_s, a_s, a_r, rs_s, rs_r, f_s, f_r):
    b = lax.axis_index("branch")
    z = lax.axis_index("tensor")
    c = lax.rem(b, 2)
    x = lax.rem(b // 2, 4)
    yh = b // 8
    chip = b // 2

    def dev(dy, dx, dc, dz=0):
        ny, nx, nc = lax.rem(yh + dy, 2), lax.rem(x + dx, 4), lax.rem(c + dc, 2)
        return {"branch": (ny * 4 + nx) * 2 + nc, "tensor": lax.rem(z + dz, TR)}

    def chip_at(dy, dx):
        return lax.rem(yh + dy, 2) * 4 + lax.rem(x + dx, 4)

    def remote(src, dst, ss, rs, to):
        return pltpu.make_async_remote_copy(src_ref=src, dst_ref=dst, send_sem=ss, recv_sem=rs,
                                            device_id=to, device_id_type=MESH)

    barrier = pltpu.get_barrier_semaphore()
    peers = [dev(0, 0, 1), dev(0, 1, 0), dev(0, 3, 0), dev(0, 2, 0), dev(1, 0, 0), dev(0, 0, 0, 1), dev(0, 0, 0, TR - 1)]
    for peer in peers:
        pl.semaphore_signal(barrier, inc=1, device_id=peer, device_id_type=MESH)

    kv[chip, c, 0:256, :] = pri_ref[0]
    kv[chip, c, 256:512, :] = fre_ref[0]
    for i in range(2):
        kv[chip, c, 512 + i * 128:640 + i * 128, :] = pri_ref[1, i * 128:(i + 1) * 128, :].astype(F32).T.astype(BF)
        kv[chip, c, 768 + i * 128:896 + i * 128, :] = fre_ref[1, i * 128:(i + 1) * 128, :].astype(F32).T.astype(BF)

    across = chip_at(1, 0)
    right, left = dev(0, 1, 0), dev(0, 3, 0)
    right_chip, left_chip, far_chip = chip_at(0, 1), chip_at(0, 3), chip_at(0, 2)
    right_across, left_across, far_across = chip_at(1, 1), chip_at(1, 3), chip_at(1, 2)
    halves = (pl.ds(0, 512), pl.ds(512, 512))

    def kv_send(i):
        to = [right, left, dev(1, 0, 0)][i]
        return remote(kv.at[chip, c], kv.at[chip, c], kv_s.at[i], kv_r.at[chip], to)

    def kv_forward(i):
        return remote(kv.at[across, c], kv.at[across, c], kf_s.at[i], kv_r.at[across], [right, left][i])

    def kv_arrival(slot):
        return remote(kv.at[slot, c], kv.at[slot, c], kv_s.at[0], kv_r.at[slot], right)

    def kv_relay(row, half):
        slot = [[left_chip, right_chip], [left_across, right_across]][row][half]
        spot = kv.at[slot, c, halves[half]]
        return remote(spot, spot, kh_s.at[row, half], kh_r.at[row, half], [right, left][half])

    def relay_arrival(row, half):
        spot = kv.at[[far_chip, far_across][row], c, halves[half]]
        return remote(spot, spot, kh_s.at[row, half], kh_r.at[row, half], right)

    def core_send(slot):
        return remote(kv.at[slot, c], kv.at[slot, c], kc_s.at[slot], kc_r.at[slot], dev(0, 0, 1))

    def core_arrival(slot):
        return remote(kv.at[slot, 1 - c], kv.at[slot, 1 - c], kc_s.at[slot], kc_r.at[slot], dev(0, 0, 1))

    own_w = yh * 2 + c
    far_w = (1 - yh) * 2 + c
    w_local = pltpu.make_async_copy(w_ref, wraw.at[own_w], wl_s.at[0])
    w_core = remote(w_ref, wraw.at[own_w], w_s.at[0], w_r.at[0], dev(0, 0, 1))

    def w_across(half):
        return remote(w_ref.at[halves[half]], wraw.at[own_w, halves[half]], w_s.at[1 + half], w_r.at[1 + half], dev(1, 0, 0))

    def w_pass(half):
        spot = wraw.at[far_w, halves[half]]
        return remote(spot, spot, w_s.at[3 + half], w_r.at[3 + half], dev(0, 0, 1))

    w_local.start()

    for j in range(CH):
        for h in range(HEADS):
            qs[j, h * ROWS:(h + 1) * ROWS, :] = q_ref[j * ROWS:(j + 1) * ROWS, h * HD:(h + 1) * HD]
    for i in range(PREFIX // 128):
        pvt[i] = pre_ref[1, i * 128:(i + 1) * 128, :].astype(F32).T.astype(BF)
    m[...] = jnp.full(m.shape, -BIG, F32)
    acc[...] = jnp.zeros(acc.shape, F32)

    def scores(keys, j):
        return dg(keys, qs[j], 1, 1)

    def with_ones(tiles):
        values = jnp.concatenate(tiles, axis=1)
        return jnp.concatenate([values, jnp.ones((16, values.shape[1]), BF)], axis=0)

    def soften(j, s, values, sections):
        old = m[j]
        new = old
        parts = []
        for start, size, penalty, limit in sections:
            sec = s[start:start + size]
            if limit is not None:
                row = lax.broadcasted_iota(jnp.int32, sec.shape, 0)
                sec = jnp.where(row <= limit, sec, -BIG)
            top = jnp.max(sec, axis=0, keepdims=True) * SCALE
            if penalty is not None:
                top = top - penalty
            new = jnp.maximum(new, top)
            parts.append((sec, penalty))
        weights = []
        for sec, penalty in parts:
            shift = new if penalty is None else new + penalty
            weights.append(jnp.exp2(sec * SCALE - shift).astype(BF))
        p = weights[0] if len(weights) == 1 else jnp.concatenate(weights, axis=0)
        m[j] = new
        acc[j] = acc[j] * jnp.exp2(old - new) + dg(values, p, 1, 0)

    def run(items):
        ahead = None
        for n, (before, keys, values, sections, j) in enumerate(items):
            if n == 0:
                before()
                ahead = scores(keys(), j)
            s = ahead
            if n + 1 < len(items):
                items[n + 1][0]()
                ahead = scores(items[n + 1][1](), items[n + 1][4])
            soften(j, s, values(), sections())

    def nothing():
        return None

    my_turn = turn_ref[b]

    def chip_keys(slot):
        return jnp.concatenate([kv[slot, 0, 0:512, :], kv[slot, 1, 0:512, :]], axis=0)

    def chip_values(slot):
        return with_ones([kv[slot, cc, 512 + 128 * i:640 + 128 * i, :] for cc in range(2) for i in range(4)])

    def chip_sections(slot, limits=None):
        out = []
        for cc in range(2):
            owner = slot * 2 + cc
            unseen = jnp.where(vis_ref[b, owner] == 1, 0.0, BIG)
            early = turn_ref[owner] < my_turn
            if limits is not None:
                early = early | (owner == b)
            later = jnp.where(early, 0.0, BIG)
            out.append((cc * 512, 256, unseen, None))
            out.append((cc * 512 + 256, 256, later, None if limits is None else limits[cc]))
        return out

    def prefix_values():
        return with_ones([pvt[i] for i in range(PREFIX // 128)])

    run([(nothing, lambda: pre_ref[0], prefix_values, lambda: [(0, PREFIX, None, None)], j) for j in range(CH)])

    pl.semaphore_wait(barrier, len(peers))
    core_send(chip).start()
    kv_send(0).start()
    kv_send(1).start()
    kv_send(2).start()
    w_core.start()
    core_arrival(chip).wait_recv()

    def own_sections(j):
        position = lax.rem(lax.broadcasted_iota(jnp.int32, (1, QT), 1), ROWS) + j * ROWS
        limits = [position + jnp.where(chip * 2 + cc == b, 0, MSG) for cc in range(2)]
        return chip_sections(chip, limits)

    def arrange(y):
        def some_rows(i, carry):
            rows = pl.ds(pl.multiple_of(i * 128, 128), 128)
            for u in range(4):
                low = wraw[y * 2, rows, u * 128:(u + 1) * 128]
                high = wraw[y * 2 + 1, rows, u * 128:(u + 1) * 128]
                w4[y, rows, u * 256:u * 256 + 128] = jnp.concatenate([low[:, :64], high[:, :64]], axis=1)
                w4[y, rows, u * 256 + 128:u * 256 + 256] = jnp.concatenate([low[:, 64:], high[:, 64:]], axis=1)
            return carry
        lax.fori_loop(0, 8, some_rows, 0)

    def chip_items(slot, sections, before=nothing):
        return [(before if j == 0 else nothing, lambda: chip_keys(slot), lambda: chip_values(slot), lambda j=j: sections(j), j)
                for j in range(CH)]

    run(chip_items(chip, own_sections))
    w_local.wait()
    w_core.wait_recv()
    arrange(yh)

    kv_arrival(right_chip).wait_recv()
    kv_relay(0, 1).start()
    core_send(right_chip).start()
    kv_arrival(left_chip).wait_recv()
    kv_relay(0, 0).start()
    core_send(left_chip).start()
    kv_arrival(across).wait_recv()
    kv_forward(0).start()
    kv_forward(1).start()
    core_send(across).start()
    for half in range(2):
        w_across(half).start()
    core_arrival(right_chip).wait_recv()

    def before_left():
        for half in range(2):
            relay_arrival(0, half).wait_recv()
        core_send(far_chip).start()
        core_arrival(left_chip).wait_recv()

    def before_across():
        core_arrival(across).wait_recv()
        kv_arrival(right_across).wait_recv()
        kv_relay(1, 1).start()
        core_send(right_across).start()
        kv_arrival(left_across).wait_recv()
        kv_relay(1, 0).start()
        core_send(left_across).start()

    run(chip_items(right_chip, lambda j: chip_sections(right_chip))
        + chip_items(left_chip, lambda j: chip_sections(left_chip), before_left)
        + chip_items(across, lambda j: chip_sections(across), before_across))

    for slot in (far_chip, right_across, left_across):
        core_arrival(slot).wait_recv()

    def a_send(j, r):
        return remote(ag.at[j, x], ag.at[j, x], a_s.at[j, r - 1], a_r.at[j, r - 1], dev(0, r, 0))

    def ring_copy(st, s, d):
        to = dev(0, 0, 0, 1 if d == 0 else TR - 1)
        return remote(sbuf.at[st, s, d], rbuf.at[st, s, d], rs_s.at[st, s, d], rs_r.at[st, s, d], to)

    def target(s, d):
        return lax.rem(z + 2 * TR - 1 - s, TR) if d == 0 else lax.rem(z + 1 + s, TR)

    def final_send(st, r):
        j, y = st // 2, lax.rem(yh + st, 2)
        spot = o_ref.at[pl.ds(pl.multiple_of(j * ROWS, ROWS), ROWS), pl.ds(pl.multiple_of((y * 4 + x) * 128, 128), 128)]
        return remote(stage.at[st, lax.rem(x + r, 4)], spot, f_s.at[st, r - 1], f_r.at[st, r - 1], dev(0, r, 0))

    def final_arrival(st, r):
        j, y = st // 2, lax.rem(yh + st, 2)
        source = lax.rem(x + 4 - r, 4)
        spot = o_ref.at[pl.ds(pl.multiple_of(j * ROWS, ROWS), ROWS), pl.ds(pl.multiple_of((y * 4 + source) * 128, 128), 128)]
        return remote(stage.at[st, 0], spot, f_s.at[st, r - 1], f_r.at[st, r - 1], dev(0, r, 0))

    def begin(st):
        j, y = st // 2, lax.rem(yh + st, 2)

        @pl.when(lax.rem(st, 2) == 0)
        def _():
            for r in (1, 3, 2):
                source = lax.rem(x + 4 - r, 4)
                remote(ag.at[j, source], ag.at[j, source], a_s.at[j, r - 1], a_r.at[j, r - 1], dev(0, r, 0)).wait_recv()

        @pl.when(st == 1)
        def _():
            w_pass(0).wait_recv()
            w_pass(1).wait_recv()
            arrange(1 - yh)

        left = ag[j].reshape(4 * ROWS, HEADS * HD)
        for u in range(4):
            product = dg(left, w4[y, :, u * 256:(u + 1) * 256], 1, 0).astype(BF)
            part[st, 2 * u] = product[:, :128]
            part[st, 2 * u + 1] = product[:, 128:]
        for d in range(2):
            sbuf[st, 0, d] = part[st, target(0, d), d * 128:(d + 1) * 128, :]
            ring_copy(st, 0, d).start()

    def middle(st, s):
        for d in range(2):
            ring_copy(st, s - 1, d).wait_recv()
            total = rbuf[st, s - 1, d].astype(F32) + part[st, target(s, d), d * 128:(d + 1) * 128, :].astype(F32)
            sbuf[st, s, d] = total.astype(BF)
            ring_copy(st, s, d).start()

    def finish(st):
        j, y = st // 2, lax.rem(yh + st, 2)
        for d in range(2):
            ring_copy(st, TR - 2, d).wait_recv()
            total = rbuf[st, TR - 2, d].astype(F32) + part[st, z, d * 128:(d + 1) * 128, :].astype(F32)
            stage[st, 2 * d:2 * d + 2] = total.astype(BF).reshape(2, ROWS, 128)
        for r in (1, 3, 2):
            final_send(st, r).start()
        o_ref[pl.ds(pl.multiple_of(j * ROWS, ROWS), ROWS), pl.ds(pl.multiple_of((y * 4 + x) * 128, 128), 128)] = stage[st, x]

    def tick(T, carry):
        def one(st, inner):
            s = T - pick(st, START)

            @pl.when(s == 0)
            def _():
                begin(st)

            @pl.when((s >= 1) & (s < TR - 1))
            def _():
                middle(st, s)

            @pl.when(s == TR - 1)
            def _():
                finish(st)

            return inner

        return lax.fori_loop(0, ST, one, carry)

    def before_second(j):
        @pl.when(j == 0)
        def _():
            for half in range(2):
                relay_arrival(1, half).wait_recv()
            core_send(far_across).start()

        @pl.when(j == CH - 1)
        def _():
            tick(0, 0)

    def before_third(j):
        return None

    def before_last(j):
        @pl.when(j == 0)
        def _():
            core_arrival(far_across).wait_recv()

        @pl.when(j == CH - 1)
        def _():
            tick(1, 0)

    def second_part(j, carry):
        def item(slot, before):
            return (lambda: before(j), lambda: chip_keys(slot), lambda: chip_values(slot), lambda: chip_sections(slot), j)

        run([item(far_chip, lambda j: None), item(left_across, before_second), item(right_across, before_third),
             item(far_across, before_last)])
        done = acc[j]
        heads = (done[:HD] / done[HD:HD + 1]).T.astype(BF)
        for h in range(HEADS):
            ag[j, x, :, h * HD:(h + 1) * HD] = heads[h * ROWS:(h + 1) * ROWS, :]
        for r in (1, 3, 2):
            a_send(j, r).start()
        for half in range(2):
            @pl.when(j == 1 + half)
            def _():
                w_across(half).wait_recv()
                w_pass(half).start()

        return carry

    lax.fori_loop(0, CH, second_part, 0)
    lax.fori_loop(2, START[-1] + TR, tick, 0)

    def drain(st, carry):
        for r in (1, 2, 3):
            final_arrival(st, r).wait_recv()
            final_send(st, r).wait_send()
        return carry

    lax.fori_loop(0, ST, drain, 0)

    def drain_ring(n, carry):
        for d in range(2):
            ring_copy(n // (TR - 1), lax.rem(n, TR - 1), d).wait_send()
        return carry

    lax.fori_loop(0, ST * (TR - 1), drain_ring, 0)

    def drain_heads(j, carry):
        for r in (1, 2, 3):
            a_send(j, r).wait_send()
        return carry

    lax.fori_loop(0, CH, drain_heads, 0)
    for i in range(3):
        kv_send(i).wait_send()
    for i in range(2):
        kv_forward(i).wait_send()
        w_across(i).wait_send()
        w_pass(i).wait_send()
        for row in range(2):
            kv_relay(row, i).wait_send()

    def drain_core(slot, carry):
        core_send(slot).wait_send()
        return carry

    lax.fori_loop(0, 8, drain_core, 0)
    w_core.wait_send()


def per_device(queries, prefix_cache, prior_cache, fresh_cache, visible, turn_order, output_weight):
    vm = pl.BlockSpec(memory_space=pltpu.VMEM)
    sm = pl.BlockSpec(memory_space=pltpu.SMEM)
    dma = pltpu.SemaphoreType.DMA
    return pl.pallas_call(
        kernel,
        name="debate",
        out_shape=jax.ShapeDtypeStruct(queries.shape, BF),
        in_specs=[vm, vm, vm, vm, sm, sm, vm],
        out_specs=vm,
        scratch_shapes=[
            pltpu.VMEM((CH, QT, HD), BF),
            pltpu.VMEM((PREFIX // 128, 128, 128), BF),
            pltpu.VMEM((8, 2, 1024, HD), BF),
            pltpu.VMEM((CH, 1, QT), F32),
            pltpu.VMEM((CH, HD + 16, QT), F32),
            pltpu.VMEM((CH, 4, ROWS, HEADS * HD), BF),
            pltpu.VMEM((4, 1024, 512), BF),
            pltpu.VMEM((2, 1024, 1024), BF),
            pltpu.VMEM((ST, TR, 4 * ROWS, 128), BF),
            pltpu.VMEM((ST, TR - 1, 2, 2 * ROWS, 128), BF),
            pltpu.VMEM((ST, TR - 1, 2, 2 * ROWS, 128), BF),
            pltpu.VMEM((ST, 4, ROWS, 128), BF),
            dma((3,)), dma((8,)), dma((2,)), dma((2, 2)), dma((2, 2)), dma((8,)), dma((8,)),
            dma((5,)), dma((5,)), dma((1,)),
            dma((CH, 3)), dma((CH, 3)),
            dma((ST, TR - 1, 2)), dma((ST, TR - 1, 2)),
            dma((ST, 3)), dma((ST, 3)),
        ],
        compiler_params=pltpu.CompilerParams(collective_id=0, has_side_effects=True, vmem_limit_bytes=60 << 20),
        cost_estimate=pl.CostEstimate(flops=15_000_000_000, bytes_accessed=6_000_000, transcendentals=20_000_000),
    )(queries, prefix_cache, prior_cache, fresh_cache, visible, turn_order, output_weight)


def solution(mesh):
    return jax.shard_map(
        per_device,
        mesh=mesh,
        in_specs=(
            P(("group", "branch"), "tensor"),
            P(None, "group", "tensor"),
            P(None, ("group", "branch"), "tensor"),
            P(None, ("group", "branch"), "tensor"),
            P("group", None),
            P("group"),
            P("tensor", "branch"),
        ),
        out_specs=P(("group", "branch"), "tensor"),
        check_vma=False,
    )
```

```python
import math

import jax
import jax.numpy as jnp
from jax import lax
from jax.experimental import pallas as pl
from jax.experimental.pallas import tpu as pltpu
from jax.sharding import PartitionSpec as P

MESH = pl.DeviceIdType.MESH
HD = 128
HEADS = 8
MSG = 256
PREFIX = 1536
CH = 4
ROWS = MSG // CH
QT = ROWS * HEADS
TR = 8
ST = 2 * CH
START = (0, 1, 2, 2, 2, 3, 3, 3)
SCALE = math.log2(math.e) / math.sqrt(HD)
BIG = 1e30
BF = jnp.bfloat16
F32 = jnp.float32


def dg(a, b, ca, cb):
    return lax.dot_general(a, b, (((ca,), (cb,)), ((), ())), preferred_element_type=F32)


def pick(index, values):
    result = jnp.int32(values[0])
    for i in range(1, len(values)):
        result = jnp.where(index == i, jnp.int32(values[i]), result)
    return result


def kernel(q_ref, pre_ref, pri_ref, fre_ref, vis_ref, turn_ref, w_ref, o_ref,
           qs, pvt, kv, m, acc, ag, wraw, w4, part, rbuf, sbuf, stage,
           kv_s, kv_r, kf_s, kh_s, kh_r, kc_s, kc_r, w_s, w_r, wl_s, a_s, a_r, rs_s, rs_r, f_s, f_r):
    b = lax.axis_index("branch")
    z = lax.axis_index("tensor")
    c = lax.rem(b, 2)
    x = lax.rem(b // 2, 4)
    yh = b // 8
    chip = b // 2

    def dev(dy, dx, dc, dz=0):
        ny, nx, nc = lax.rem(yh + dy, 2), lax.rem(x + dx, 4), lax.rem(c + dc, 2)
        return {"branch": (ny * 4 + nx) * 2 + nc, "tensor": lax.rem(z + dz, TR)}

    def chip_at(dy, dx):
        return lax.rem(yh + dy, 2) * 4 + lax.rem(x + dx, 4)

    def remote(src, dst, ss, rs, to):
        return pltpu.make_async_remote_copy(src_ref=src, dst_ref=dst, send_sem=ss, recv_sem=rs,
                                            device_id=to, device_id_type=MESH)

    barrier = pltpu.get_barrier_semaphore()
    peers = [dev(0, 0, 1), dev(0, 1, 0), dev(0, 3, 0), dev(0, 2, 0), dev(1, 0, 0), dev(0, 0, 0, 1), dev(0, 0, 0, TR - 1)]
    for peer in peers:
        pl.semaphore_signal(barrier, inc=1, device_id=peer, device_id_type=MESH)

    kv[chip, c, 0:256, :] = pri_ref[0]
    kv[chip, c, 256:512, :] = fre_ref[0]
    for i in range(2):
        kv[chip, c, 512 + i * 128:640 + i * 128, :] = pri_ref[1, i * 128:(i + 1) * 128, :].astype(F32).T.astype(BF)
        kv[chip, c, 768 + i * 128:896 + i * 128, :] = fre_ref[1, i * 128:(i + 1) * 128, :].astype(F32).T.astype(BF)

    across = chip_at(1, 0)
    right, left = dev(0, 1, 0), dev(0, 3, 0)
    right_chip, left_chip, far_chip = chip_at(0, 1), chip_at(0, 3), chip_at(0, 2)
    right_across, left_across, far_across = chip_at(1, 1), chip_at(1, 3), chip_at(1, 2)
    halves = (pl.ds(0, 512), pl.ds(512, 512))

    def kv_send(i):
        to = [right, left, dev(1, 0, 0)][i]
        return remote(kv.at[chip, c], kv.at[chip, c], kv_s.at[i], kv_r.at[chip], to)

    def kv_forward(i):
        return remote(kv.at[across, c], kv.at[across, c], kf_s.at[i], kv_r.at[across], [right, left][i])

    def kv_arrival(slot):
        return remote(kv.at[slot, c], kv.at[slot, c], kv_s.at[0], kv_r.at[slot], right)

    def kv_relay(row, half):
        slot = [[left_chip, right_chip], [left_across, right_across]][row][half]
        spot = kv.at[slot, c, halves[half]]
        return remote(spot, spot, kh_s.at[row, half], kh_r.at[row, half], [right, left][half])

    def relay_arrival(row, half):
        spot = kv.at[[far_chip, far_across][row], c, halves[half]]
        return remote(spot, spot, kh_s.at[row, half], kh_r.at[row, half], right)

    def core_send(slot):
        return remote(kv.at[slot, c], kv.at[slot, c], kc_s.at[slot], kc_r.at[slot], dev(0, 0, 1))

    def core_arrival(slot):
        return remote(kv.at[slot, 1 - c], kv.at[slot, 1 - c], kc_s.at[slot], kc_r.at[slot], dev(0, 0, 1))

    own_w = yh * 2 + c
    far_w = (1 - yh) * 2 + c
    w_local = pltpu.make_async_copy(w_ref, wraw.at[own_w], wl_s.at[0])
    w_core = remote(w_ref, wraw.at[own_w], w_s.at[0], w_r.at[0], dev(0, 0, 1))

    def w_across(half):
        return remote(w_ref.at[halves[half]], wraw.at[own_w, halves[half]], w_s.at[1 + half], w_r.at[1 + half], dev(1, 0, 0))

    def w_pass(half):
        spot = wraw.at[far_w, halves[half]]
        return remote(spot, spot, w_s.at[3 + half], w_r.at[3 + half], dev(0, 0, 1))

    w_local.start()

    for j in range(CH):
        for h in range(HEADS):
            qs[j, h * ROWS:(h + 1) * ROWS, :] = q_ref[j * ROWS:(j + 1) * ROWS, h * HD:(h + 1) * HD]
    for i in range(PREFIX // 128):
        pvt[i] = pre_ref[1, i * 128:(i + 1) * 128, :].astype(F32).T.astype(BF)
    m[...] = jnp.full(m.shape, -BIG, F32)
    acc[...] = jnp.zeros(acc.shape, F32)

    def scores(keys, j):
        return dg(keys, qs[j], 1, 1)

    def with_ones(tiles):
        values = jnp.concatenate(tiles, axis=1)
        return jnp.concatenate([values, jnp.ones((16, values.shape[1]), BF)], axis=0)

    def soften(j, s, values, sections):
        old = m[j]
        new = old
        parts = []
        for start, size, penalty, limit in sections:
            sec = s[start:start + size]
            if limit is not None:
                row = lax.broadcasted_iota(jnp.int32, sec.shape, 0)
                sec = jnp.where(row <= limit, sec, -BIG)
            top = jnp.max(sec, axis=0, keepdims=True) * SCALE
            if penalty is not None:
                top = top - penalty
            new = jnp.maximum(new, top)
            parts.append((sec, penalty))
        weights = []
        for sec, penalty in parts:
            shift = new if penalty is None else new + penalty
            weights.append(jnp.exp2(sec * SCALE - shift).astype(BF))
        p = weights[0] if len(weights) == 1 else jnp.concatenate(weights, axis=0)
        m[j] = new
        acc[j] = acc[j] * jnp.exp2(old - new) + dg(values, p, 1, 0)

    def run(items):
        ahead = None
        for n, (before, keys, values, sections, j) in enumerate(items):
            if n == 0:
                before()
                ahead = scores(keys(), j)
            s = ahead
            if n + 1 < len(items):
                items[n + 1][0]()
                ahead = scores(items[n + 1][1](), items[n + 1][4])
            soften(j, s, values(), sections())

    def nothing():
        return None

    my_turn = turn_ref[b]

    def chip_keys(slot):
        return jnp.concatenate([kv[slot, 0, 0:512, :], kv[slot, 1, 0:512, :]], axis=0)

    def chip_values(slot):
        return with_ones([kv[slot, cc, 512 + 128 * i:640 + 128 * i, :] for cc in range(2) for i in range(4)])

    def chip_sections(slot, limits=None):
        out = []
        for cc in range(2):
            owner = slot * 2 + cc
            unseen = jnp.where(vis_ref[b, owner] == 1, 0.0, BIG)
            early = turn_ref[owner] < my_turn
            if limits is not None:
                early = early | (owner == b)
            later = jnp.where(early, 0.0, BIG)
            out.append((cc * 512, 256, unseen, None))
            out.append((cc * 512 + 256, 256, later, None if limits is None else limits[cc]))
        return out

    def prefix_values():
        return with_ones([pvt[i] for i in range(PREFIX // 128)])

    run([(nothing, lambda: pre_ref[0], prefix_values, lambda: [(0, PREFIX, None, None)], j) for j in range(CH)])

    pl.semaphore_wait(barrier, len(peers))
    core_send(chip).start()
    kv_send(0).start()
    kv_send(1).start()
    kv_send(2).start()
    w_core.start()
    core_arrival(chip).wait_recv()

    def own_sections(j):
        position = lax.rem(lax.broadcasted_iota(jnp.int32, (1, QT), 1), ROWS) + j * ROWS
        limits = [position + jnp.where(chip * 2 + cc == b, 0, MSG) for cc in range(2)]
        return chip_sections(chip, limits)

    def arrange(y):
        def some_rows(i, carry):
            rows = pl.ds(pl.multiple_of(i * 128, 128), 128)
            for u in range(4):
                low = wraw[y * 2, rows, u * 128:(u + 1) * 128]
                high = wraw[y * 2 + 1, rows, u * 128:(u + 1) * 128]
                w4[y, rows, u * 256:u * 256 + 128] = jnp.concatenate([low[:, :64], high[:, :64]], axis=1)
                w4[y, rows, u * 256 + 128:u * 256 + 256] = jnp.concatenate([low[:, 64:], high[:, 64:]], axis=1)
            return carry
        lax.fori_loop(0, 8, some_rows, 0)

    def chip_items(slot, sections, before=nothing):
        return [(before if j == 0 else nothing, lambda: chip_keys(slot), lambda: chip_values(slot), lambda j=j: sections(j), j)
                for j in range(CH)]

    run(chip_items(chip, own_sections))
    kv_arrival(across).wait_recv()
    kv_forward(0).start()
    kv_forward(1).start()
    kv_arrival(right_chip).wait_recv()
    core_send(right_chip).start()
    kv_arrival(left_chip).wait_recv()
    core_send(left_chip).start()
    core_send(across).start()
    for half in range(2):
        w_across(half).start()
    w_local.wait()
    w_core.wait_recv()
    arrange(yh)
    core_arrival(right_chip).wait_recv()

    def before_left():
        for half in range(2):
            kv_relay(0, half).start()
        core_arrival(left_chip).wait_recv()

    def far_arrives():
        for half in range(2):
            relay_arrival(0, half).wait_recv()
        core_send(far_chip).start()

    def before_across():
        core_arrival(across).wait_recv()
        kv_arrival(right_across).wait_recv()
        kv_relay(1, 1).start()
        core_send(right_across).start()
        kv_arrival(left_across).wait_recv()
        kv_relay(1, 0).start()
        core_send(left_across).start()

    across_items = chip_items(across, lambda j: chip_sections(across), before_across)
    across_items[2] = (far_arrives,) + across_items[2][1:]
    run(chip_items(right_chip, lambda j: chip_sections(right_chip))
        + chip_items(left_chip, lambda j: chip_sections(left_chip), before_left)
        + across_items)

    for slot in (right_across, left_across):
        core_arrival(slot).wait_recv()

    def a_send(j, r):
        return remote(ag.at[j, x], ag.at[j, x], a_s.at[j, r - 1], a_r.at[j, r - 1], dev(0, r, 0))

    def ring_copy(st, s, d):
        to = dev(0, 0, 0, 1 if d == 0 else TR - 1)
        return remote(sbuf.at[st, s, d], rbuf.at[st, s, d], rs_s.at[st, s, d], rs_r.at[st, s, d], to)

    def target(s, d):
        return lax.rem(z + 2 * TR - 1 - s, TR) if d == 0 else lax.rem(z + 1 + s, TR)

    def final_send(st, r):
        j, y = st // 2, lax.rem(yh + st, 2)
        spot = o_ref.at[pl.ds(pl.multiple_of(j * ROWS, ROWS), ROWS), pl.ds(pl.multiple_of((y * 4 + x) * 128, 128), 128)]
        return remote(stage.at[st, lax.rem(x + r, 4)], spot, f_s.at[st, r - 1], f_r.at[st, r - 1], dev(0, r, 0))

    def final_arrival(st, r):
        j, y = st // 2, lax.rem(yh + st, 2)
        source = lax.rem(x + 4 - r, 4)
        spot = o_ref.at[pl.ds(pl.multiple_of(j * ROWS, ROWS), ROWS), pl.ds(pl.multiple_of((y * 4 + source) * 128, 128), 128)]
        return remote(stage.at[st, 0], spot, f_s.at[st, r - 1], f_r.at[st, r - 1], dev(0, r, 0))

    def begin(st):
        j, y = st // 2, lax.rem(yh + st, 2)

        @pl.when(lax.rem(st, 2) == 0)
        def _():
            for r in (1, 3, 2):
                source = lax.rem(x + 4 - r, 4)
                remote(ag.at[j, source], ag.at[j, source], a_s.at[j, r - 1], a_r.at[j, r - 1], dev(0, r, 0)).wait_recv()

        @pl.when(st == 1)
        def _():
            w_pass(0).wait_recv()
            w_pass(1).wait_recv()
            arrange(1 - yh)

        left = ag[j].reshape(4 * ROWS, HEADS * HD)
        for u in range(4):
            product = dg(left, w4[y, :, u * 256:(u + 1) * 256], 1, 0).astype(BF)
            part[st, 2 * u] = product[:, :128]
            part[st, 2 * u + 1] = product[:, 128:]
        for d in range(2):
            sbuf[st, 0, d] = part[st, target(0, d), d * 128:(d + 1) * 128, :]
            ring_copy(st, 0, d).start()

    def middle(st, s):
        for d in range(2):
            ring_copy(st, s - 1, d).wait_recv()
            total = rbuf[st, s - 1, d].astype(F32) + part[st, target(s, d), d * 128:(d + 1) * 128, :].astype(F32)
            sbuf[st, s, d] = total.astype(BF)
            ring_copy(st, s, d).start()

    def finish(st):
        j, y = st // 2, lax.rem(yh + st, 2)
        for d in range(2):
            ring_copy(st, TR - 2, d).wait_recv()
            total = rbuf[st, TR - 2, d].astype(F32) + part[st, z, d * 128:(d + 1) * 128, :].astype(F32)
            stage[st, 2 * d:2 * d + 2] = total.astype(BF).reshape(2, ROWS, 128)
        for r in (1, 3, 2):
            final_send(st, r).start()
        o_ref[pl.ds(pl.multiple_of(j * ROWS, ROWS), ROWS), pl.ds(pl.multiple_of((y * 4 + x) * 128, 128), 128)] = stage[st, x]

    def tick(T, carry):
        def one(st, inner):
            s = T - pick(st, START)

            @pl.when(s == 0)
            def _():
                begin(st)

            @pl.when((s >= 1) & (s < TR - 1))
            def _():
                middle(st, s)

            @pl.when(s == TR - 1)
            def _():
                finish(st)

            return inner

        return lax.fori_loop(0, ST, one, carry)

    def before_second(j):
        @pl.when(j == 0)
        def _():
            for half in range(2):
                relay_arrival(1, half).wait_recv()
            core_send(far_across).start()

        @pl.when(j == CH - 1)
        def _():
            tick(0, 0)

    def before_third(j):
        @pl.when(j == 0)
        def _():
            core_arrival(far_chip).wait_recv()

    def before_last(j):
        @pl.when(j == 0)
        def _():
            core_arrival(far_across).wait_recv()

        @pl.when(j == CH - 1)
        def _():
            tick(1, 0)

    def second_part(j, carry):
        def item(slot, before):
            return (lambda: before(j), lambda: chip_keys(slot), lambda: chip_values(slot), lambda: chip_sections(slot), j)

        run([item(left_across, lambda j: None), item(right_across, before_second), item(far_chip, before_third),
             item(far_across, before_last)])
        done = acc[j]
        heads = (done[:HD] / done[HD:HD + 1]).T.astype(BF)
        for h in range(HEADS):
            ag[j, x, :, h * HD:(h + 1) * HD] = heads[h * ROWS:(h + 1) * ROWS, :]
        for r in (1, 3, 2):
            a_send(j, r).start()
        for half in range(2):
            @pl.when(j == 1 + half)
            def _():
                w_across(half).wait_recv()
                w_pass(half).start()

        return carry

    lax.fori_loop(0, CH, second_part, 0)
    lax.fori_loop(2, START[-1] + TR, tick, 0)

    def drain(st, carry):
        for r in (1, 2, 3):
            final_arrival(st, r).wait_recv()
            final_send(st, r).wait_send()
        return carry

    lax.fori_loop(0, ST, drain, 0)

    def drain_ring(n, carry):
        for d in range(2):
            ring_copy(n // (TR - 1), lax.rem(n, TR - 1), d).wait_send()
        return carry

    lax.fori_loop(0, ST * (TR - 1), drain_ring, 0)

    def drain_heads(j, carry):
        for r in (1, 2, 3):
            a_send(j, r).wait_send()
        return carry

    lax.fori_loop(0, CH, drain_heads, 0)
    for i in range(3):
        kv_send(i).wait_send()
    for i in range(2):
        kv_forward(i).wait_send()
        w_across(i).wait_send()
        w_pass(i).wait_send()
        for row in range(2):
            kv_relay(row, i).wait_send()

    def drain_core(slot, carry):
        core_send(slot).wait_send()
        return carry

    lax.fori_loop(0, 8, drain_core, 0)
    w_core.wait_send()


def per_device(queries, prefix_cache, prior_cache, fresh_cache, visible, turn_order, output_weight):
    vm = pl.BlockSpec(memory_space=pltpu.VMEM)
    sm = pl.BlockSpec(memory_space=pltpu.SMEM)
    dma = pltpu.SemaphoreType.DMA
    return pl.pallas_call(
        kernel,
        name="debate",
        out_shape=jax.ShapeDtypeStruct(queries.shape, BF),
        in_specs=[vm, vm, vm, vm, sm, sm, vm],
        out_specs=vm,
        scratch_shapes=[
            pltpu.VMEM((CH, QT, HD), BF),
            pltpu.VMEM((PREFIX // 128, 128, 128), BF),
            pltpu.VMEM((8, 2, 1024, HD), BF),
            pltpu.VMEM((CH, 1, QT), F32),
            pltpu.VMEM((CH, HD + 16, QT), F32),
            pltpu.VMEM((CH, 4, ROWS, HEADS * HD), BF),
            pltpu.VMEM((4, 1024, 512), BF),
            pltpu.VMEM((2, 1024, 1024), BF),
            pltpu.VMEM((ST, TR, 4 * ROWS, 128), BF),
            pltpu.VMEM((ST, TR - 1, 2, 2 * ROWS, 128), BF),
            pltpu.VMEM((ST, TR - 1, 2, 2 * ROWS, 128), BF),
            pltpu.VMEM((ST, 4, ROWS, 128), BF),
            dma((3,)), dma((8,)), dma((2,)), dma((2, 2)), dma((2, 2)), dma((8,)), dma((8,)),
            dma((5,)), dma((5,)), dma((1,)),
            dma((CH, 3)), dma((CH, 3)),
            dma((ST, TR - 1, 2)), dma((ST, TR - 1, 2)),
            dma((ST, 3)), dma((ST, 3)),
        ],
        compiler_params=pltpu.CompilerParams(collective_id=0, has_side_effects=True, vmem_limit_bytes=60 << 20),
        cost_estimate=pl.CostEstimate(flops=15_000_000_000, bytes_accessed=6_000_000, transcendentals=20_000_000),
    )(queries, prefix_cache, prior_cache, fresh_cache, visible, turn_order, output_weight)


def solution(mesh):
    return jax.shard_map(
        per_device,
        mesh=mesh,
        in_specs=(
            P(("group", "branch"), "tensor"),
            P(None, "group", "tensor"),
            P(None, ("group", "branch"), "tensor"),
            P(None, ("group", "branch"), "tensor"),
            P("group", None),
            P("group"),
            P("tensor", "branch"),
        ),
        out_specs=P(("group", "branch"), "tensor"),
        check_vma=False,
    )
```
